32 devices in a mesh: dp: 4 (over y, core), fsdp: 4 (over z), seq: 2 (over x).
Axes of the slice: x: 2, y: 2, z: 4, core: 2. Of those that a mesh axis runs over, the one named last changes fastest.
Arguments:
- queries: bfloat16 [16, 256, 2048], P(('dp', 'fsdp'), 'seq'), may hold values from -30 to 30
- key_rows: bfloat16 [16, 256, 2048], P(('dp', 'fsdp'), 'seq'), may hold values from -12 to 12
- value_rows: bfloat16 [16, 256, 2048], P(('dp', 'fsdp'), 'seq'), may hold values from -6 to 6
- cotangent: bfloat16 [16, 256, 2048], P(('dp', 'fsdp'), 'seq'), may hold values from -6 to 6
- out_weight: bfloat16 [2048, 2048], P('fsdp'), may hold values from -0.125 to 0.125
Outputs:
- query_grad: bfloat16 [16, 256, 2048], P(('dp', 'fsdp'), 'seq')
- key_grad: bfloat16 [16, 256, 2048], P(('dp', 'fsdp'), 'seq')
- value_grad: bfloat16 [16, 256, 2048], P(('dp', 'fsdp'), 'seq')
- weight_grad: float32 [2048, 2048], P('fsdp')
The draws below stay inside these ranges and needn't reach their ends.
All inputs are finite; a program needn't handle non-finite values.
Results may differ from the reference program's by a relative error of at most 0.014.
Values may be sent and summed in bfloat16 or wider, within the bound.
A program may use at most 128 MiB of HBM per device.

```python
import jax
import jax.numpy as jnp
from jax import lax

D = 2048
H = 16
DH = 128
HD = 2048
SEQ_LEN = 256
SAMPLES = 16


def base_rows(key, salt):
    shape = (SAMPLES, SEQ_LEN, H * DH)
    entries = jnp.clip(jax.random.normal(jax.random.fold_in(key, salt), shape, jnp.float32), -4.0, 4.0)
    lows = jax.random.uniform(jax.random.fold_in(key, salt + 50), (SAMPLES, SEQ_LEN, 1), jnp.float32, jnp.log(0.3), jnp.log(3.0))
    return entries * jnp.exp(lows)


def draw_queries(key, part):
    base = base_rows(key, 21)
    return base.astype(jnp.bfloat16)


def draw_key_rows(key, part):
    base = base_rows(key, 22)
    return base.astype(jnp.bfloat16)


def steps_of(rng, extent, cuts, low, top_value):
    factor_of, own = 1.0, jax.random.fold_in(rng, 6)
    for position, parts in cuts:
        heights = jnp.exp(jax.random.uniform(jax.random.fold_in(own, position), (parts,), jnp.float32, low / len(cuts), top_value / len(cuts)))
        factor_of = factor_of * jnp.repeat(heights, extent[position] // parts).reshape([-1 if axis == position else 1 for axis in range(len(extent))])
    return factor_of


def centred(own_key, extent, spread, limit, split=(), kind=jnp.bfloat16):
    values = jax.random.normal(own_key, extent, jnp.float32) * spread
    if len(split) > 0:
        values = steps_of(own_key, extent, split, -0.22, 0.18) * values
    return jnp.clip(values, min=-limit, max=limit).astype(kind)


def setup_inputs(seed: int = 0) -> dict:
    key_of = jax.random.split(jax.random.key(seed), 6)
    return {
        "queries": draw_queries(jax.random.fold_in(key_of[5], 71), 0),
        "key_rows": draw_key_rows(jax.random.fold_in(key_of[5], 71), 0),
        "value_rows": centred(key_of[2], (SAMPLES, SEQ_LEN, HD), 1.0, 6.0, ((0, 16), (1, 2))),
        "cotangent": centred(key_of[3], (SAMPLES, SEQ_LEN, D), 1.0, 6.0, ((0, 16), (1, 2))),
        "out_weight": centred(key_of[4], (HD, D), HD ** -0.5, 0.125, ((0, 4),)),
    }


def head_backward(query_head, key_head, value_head, grad_head):
    score_scale = DH ** -0.5
    query_f = query_head.astype(jnp.float32)
    key_f = key_head.astype(jnp.float32)
    value_f = value_head.astype(jnp.float32)
    grad_f = grad_head.astype(jnp.float32)
    scores = jnp.dot(query_f, key_f.T) * score_scale
    highest = jnp.max(scores, axis=1, keepdims=True)
    expanded = jnp.exp(scores - highest)
    weights = expanded / jnp.sum(expanded, axis=1, keepdims=True)
    weights_half = weights.astype(jnp.bfloat16)
    weights_back = weights_half.astype(jnp.float32)
    attended = jnp.dot(weights_back, value_f).astype(jnp.bfloat16)
    grad_weights = jnp.dot(grad_f, value_f.T)
    row_delta = jnp.sum(weights * grad_weights, axis=1, keepdims=True)
    grad_scores = (weights * (grad_weights - row_delta)).astype(jnp.bfloat16).astype(jnp.float32)
    query_grad = (jnp.dot(grad_scores, key_f) * score_scale).astype(jnp.bfloat16)
    key_grad = (jnp.dot(grad_scores.T, query_f) * score_scale).astype(jnp.bfloat16)
    value_grad = jnp.dot(weights_back.T, grad_f).astype(jnp.bfloat16)
    return attended, query_grad, key_grad, value_grad


def split_heads(array):
    return array.reshape(SAMPLES, SEQ_LEN, H, DH).transpose(0, 2, 1, 3).reshape(SAMPLES * H, SEQ_LEN, DH)


def join_heads(array):
    return array.reshape(SAMPLES, H, SEQ_LEN, DH).transpose(0, 2, 1, 3).reshape(SAMPLES, SEQ_LEN, H * DH)


def reference(queries, key_rows, value_rows, cotangent, out_weight):
    flat_cot = cotangent.reshape(SAMPLES * SEQ_LEN, D).astype(jnp.float32)
    grad_out = jnp.dot(flat_cot, out_weight.astype(jnp.float32).T).astype(jnp.bfloat16)
    grad_out = grad_out.reshape(SAMPLES, SEQ_LEN, H * DH)
    stacked = (split_heads(queries), split_heads(key_rows), split_heads(value_rows), split_heads(grad_out))
    attended, query_grad, key_grad, value_grad = lax.map(lambda group: head_backward(*group), stacked)
    attended = join_heads(attended)
    flat_att = attended.reshape(SAMPLES * SEQ_LEN, H * DH).astype(jnp.float32)
    weight_grad = jnp.dot(flat_att.T, flat_cot) / SAMPLES
    return join_heads(query_grad), join_heads(key_grad), join_heads(value_grad), weight_grad
```

```python
import functools

import jax
import jax.numpy as jnp
from jax import lax
from jax.experimental import pallas as pl
from jax.experimental.pallas import tpu as pltpu
from jax.sharding import PartitionSpec as P

DH = 128
CHUNKS = 4
F32 = jnp.float32
BF16 = jnp.bfloat16


def head_backward(query_head, key_head, value_head, grad_head, block_rows):
    length = key_head.shape[0]
    score_scale = DH ** (-0.5)
    blocks = length // block_rows

    def visit(carry, block):
        key_acc, value_acc = carry
        begin = block * block_rows
        query_block = lax.dynamic_slice_in_dim(query_head, begin, block_rows, 0)
        grad_block = lax.dynamic_slice_in_dim(grad_head, begin, block_rows, 0)
        scores = (
            jnp.einsum("qd,kd->qk", query_block, key_head, preferred_element_type=jnp.float32)
            * score_scale
        )
        highest = jnp.max(scores, axis=1, keepdims=True)
        expanded = jnp.exp(scores - highest)
        weights = expanded / jnp.sum(expanded, axis=1, keepdims=True)
        weights_half = weights.astype(jnp.bfloat16)
        attended = jnp.einsum(
            "qk,kd->qd", weights_half, value_head, preferred_element_type=jnp.float32
        ).astype(jnp.bfloat16)
        grad_weights = jnp.einsum(
            "qd,kd->qk", grad_block, value_head, preferred_element_type=jnp.float32
        )
        row_delta = jnp.sum(weights * grad_weights, axis=1, keepdims=True)
        grad_scores = (weights * (grad_weights - row_delta)).astype(jnp.bfloat16)
        query_grad = (
            jnp.einsum("qk,kd->qd", grad_scores, key_head, preferred_element_type=jnp.float32)
            * score_scale
        ).astype(jnp.bfloat16)
        key_acc = key_acc + jnp.einsum(
            "qk,qd->kd", grad_scores, query_block, preferred_element_type=jnp.float32
        )
        value_acc = value_acc + jnp.einsum(
            "qk,qd->kd", weights_half, grad_block, preferred_element_type=jnp.float32
        )
        return ((key_acc, value_acc), (attended, query_grad))

    empty = jnp.zeros(key_head.shape, jnp.float32)
    finals, stacked = lax.scan(visit, (empty, empty), jnp.arange(blocks))
    attended = stacked[0].reshape(length, DH)
    query_grad = stacked[1].reshape(length, DH)
    key_grad = (finals[0] * score_scale).astype(jnp.bfloat16)
    value_grad = finals[1].astype(jnp.bfloat16)
    return (attended, query_grad, key_grad, value_grad)


def attend_heads(query_heads, key_heads, value_heads, grad_heads):
    length = query_heads.shape[1]
    per_device = query_heads.shape[2] // DH
    block_rows = min(512, length)
    gathered = [[], [], [], []]
    for head_index in range(per_device):
        lower = head_index * DH
        upper = lower + DH
        results = head_backward(
            query_heads[0, :, lower:upper],
            key_heads[0, :, lower:upper],
            value_heads[0, :, lower:upper],
            grad_heads[0, :, lower:upper],
            block_rows,
        )
        for position, result in enumerate(results):
            gathered[position].append(result)
    return tuple((jnp.concatenate(group, axis=1)[None] for group in gathered))


def body(queries, key_rows, value_rows, cotangent, out_weight):
    samples = lax.axis_size("dp") * lax.axis_size("fsdp")
    grad_out = jnp.einsum(
        "btd,rd->btr",
        cotangent,
        lax.all_gather(out_weight, "fsdp", axis=0, tiled=True),
        preferred_element_type=jnp.float32,
    ).astype(jnp.bfloat16)
    query_heads, key_heads, value_heads, grad_heads = (
        lax.all_to_all(queries, "seq", split_axis=2, concat_axis=1, tiled=True),
        lax.all_to_all(key_rows, "seq", split_axis=2, concat_axis=1, tiled=True),
        lax.all_to_all(value_rows, "seq", split_axis=2, concat_axis=1, tiled=True),
        lax.all_to_all(grad_out, "seq", split_axis=2, concat_axis=1, tiled=True),
    )
    head_results = attend_heads(query_heads, key_heads, value_heads, grad_heads)
    attended, query_grad, key_grad, value_grad = (
        lax.all_to_all(head_results[0], "seq", split_axis=1, concat_axis=2, tiled=True),
        lax.all_to_all(head_results[1], "seq", split_axis=1, concat_axis=2, tiled=True),
        lax.all_to_all(head_results[2], "seq", split_axis=1, concat_axis=2, tiled=True),
        lax.all_to_all(head_results[3], "seq", split_axis=1, concat_axis=2, tiled=True),
    )
    shares = lax.psum_scatter(
        jnp.einsum("btr,btd->rd", attended, cotangent, preferred_element_type=jnp.float32),
        ("fsdp", "seq"),
        scatter_dimension=0,
        tiled=True,
    )
    shares = lax.psum(shares.astype(jnp.bfloat16), "dp").astype(jnp.float32)
    total = lax.all_gather(shares.astype(jnp.bfloat16), "seq", axis=0, tiled=True).astype(
        shares.dtype
    )
    return (query_grad, key_grad, value_grad, total / samples)


def dot_nn(a, b):
    return lax.dot_general(a, b, (((1,), (0,)), ((), ())), preferred_element_type=F32)


def dot_nt(a, b):
    return lax.dot_general(a, b, (((1,), (1,)), ((), ())), preferred_element_type=F32)


def dot_tn(a, b):
    return lax.dot_general(a, b, (((0,), (0,)), ((), ())), preferred_element_type=F32)


def fused_kernel(
    nf,
    q_ref,
    k_ref,
    v_ref,
    c_ref,
    w_ref,
    qg_ref,
    kg_ref,
    vg_ref,
    wg_ref,
    cot,
    keys,
    vals,
    go_out,
    go_in,
    at_out,
    at_in,
    probs,
    kv_out,
    kv_in,
    kv_own,
    acc,
    core_out,
    core_in,
    y_out,
    y_in,
    x_out,
    x_in,
    final,
    cot_send,
    cot_recv,
    pair_send,
    pair_recv,
    go_send,
    go_recv,
    at_send,
    at_recv,
    kv_send,
    kv_recv,
    rs_send,
    rs_recv,
    ag_send,
    ag_recv,
):
    tokens, width = c_ref.shape
    rows = w_ref.shape[0]
    group_heads = rows // DH
    scale = DH ** (-0.5)
    dp = lax.axis_index("dp")
    f = lax.axis_index("fsdp")
    s = lax.axis_index("seq")
    core = dp % 2
    half = dp // 2
    sibling = {"dp": half * 2 + (1 - core)}
    across = {"dp": (1 - half) * 2 + core}
    partner = {"seq": 1 - s}

    def remote(src, dst, send, recv, device):
        return pltpu.make_async_remote_copy(
            src_ref=src,
            dst_ref=dst,
            send_sem=send,
            recv_sem=recv,
            device_id=device,
            device_id_type=pl.DeviceIdType.MESH,
        )

    barrier = pltpu.get_barrier_semaphore()
    for device in (sibling, across, partner):
        pl.semaphore_signal(
            barrier, inc=1, device_id=device, device_id_type=pl.DeviceIdType.MESH
        )
    for step in range(1, nf):
        pl.semaphore_signal(
            barrier,
            inc=1,
            device_id={"fsdp": (f + step) % nf},
            device_id_type=pl.DeviceIdType.MESH,
        )
    pl.semaphore_wait(barrier, 3 + nf - 1)

    def cot_up(j):
        return remote(cot.at[j], cot.at[j], cot_send.at[0, j], cot_recv.at[j], {"fsdp": f + 1})

    def cot_down(j):
        return remote(cot.at[j], cot.at[j], cot_send.at[1, j], cot_recv.at[j], {"fsdp": f - 1})

    def go_copy(j, peer):
        return remote(go_out.at[j], go_in.at[f], go_send.at[j], go_recv.at[f], {"fsdp": peer})

    def at_copy(j, peer):
        return remote(at_out.at[j], at_in.at[f], at_send.at[j], at_recv.at[f], {"fsdp": peer})

    def kv_copy(which, g):
        return remote(
            kv_out.at[which, g],
            kv_in.at[which, g],
            kv_send.at[which, g],
            kv_recv.at[which, g],
            partner,
        )

    def wait_into(ref, sem):
        pltpu.make_async_copy(ref, ref, sem).wait()

    cot[f] = c_ref[...]

    @pl.when(f + 1 < nf)
    def _():
        cot_up(f).start()

    @pl.when(f > 0)
    def _():
        cot_down(f).start()

    keys[0] = k_ref[...]
    vals[0] = v_ref[...]
    key_copy = remote(keys.at[0], keys.at[1], pair_send.at[0], pair_recv.at[0], partner)
    val_copy = remote(vals.at[0], vals.at[1], pair_send.at[1], pair_recv.at[1], partner)
    key_copy.start()
    val_copy.start()

    def project(j):
        return dot_nt(cot[j], w_ref[...]).astype(BF16)

    go_in[f] = project(f)

    def visit_peers(first, last, action):
        def step(i, carry):
            d = i // 2
            j = f + d * (1 - 2 * (i % 2))

            @pl.when((j >= 0) & (j < nf))
            def _():
                action(j)

            return carry

        lax.fori_loop(2 * first, 2 * last, step, 0)

    def take_cot(j):
        wait_into(cot.at[j], cot_recv.at[j])

        @pl.when((j < f) & (f + 1 < nf))
        def _():
            cot_up(j).start()

        @pl.when((j > f) & (f > 0))
        def _():
            cot_down(j).start()

        go_out[j] = project(j)
        go_copy(j, j).start()

    visit_peers(1, nf - 1, take_cot)

    key_copy.wait()
    val_copy.wait()

    def soften(g, carry):
        base = g * rows
        for t in range(group_heads):
            cols = pl.ds(pl.multiple_of(base + t * DH, DH), DH)
            kh = keys[:, :, cols].reshape(2 * tokens, DH)
            vh = vals[:, :, cols].reshape(2 * tokens, DH)
            scores = dot_nt(q_ref[:, cols], kh) * scale
            highest = jnp.max(scores, axis=1, keepdims=True)
            expanded = jnp.exp(scores - highest)
            weights = expanded / jnp.sum(expanded, axis=1, keepdims=True)
            probs[g * group_heads + t] = weights
            at_out[g, :, t * DH : (t + 1) * DH] = dot_nn(weights.astype(BF16), vh).astype(BF16)

        @pl.when(g == f)
        def _():
            at_in[f] = at_out[f]

        @pl.when(g != f)
        def _():
            at_copy(g, g).start()

        return carry

    lax.fori_loop(0, nf, soften, 0)

    def differentiate(g):
        base = g * rows
        for t in range(group_heads):
            cols = pl.ds(pl.multiple_of(base + t * DH, DH), DH)
            inner = slice(t * DH, (t + 1) * DH)
            kh = keys[:, :, cols].reshape(2 * tokens, DH)
            vh = vals[:, :, cols].reshape(2 * tokens, DH)
            qh = q_ref[:, cols]
            gh = go_in[g, :, inner]
            weights = probs[g * group_heads + t]
            grad_weights = dot_nt(gh, vh)
            delta = jnp.sum(weights * grad_weights, axis=1, keepdims=True)
            grad_scores = (weights * (grad_weights - delta)).astype(BF16)
            qg_ref[:, cols] = (dot_nn(grad_scores, kh) * scale).astype(BF16)
            kg = dot_tn(grad_scores, qh) * scale
            vg = dot_tn(weights.astype(BF16), gh)
            kv_own[0, g, :, inner] = kg[:tokens]
            kv_own[1, g, :, inner] = vg[:tokens]
            kv_out[0, g, :, inner] = kg[tokens:].astype(BF16)
            kv_out[1, g, :, inner] = vg[tokens:].astype(BF16)
        kv_copy(0, g).start()
        kv_copy(1, g).start()

    def take_go(j):
        wait_into(go_in.at[j], go_recv.at[j])
        differentiate(j)

    differentiate(f)
    visit_peers(nf - 1, nf, take_cot)
    visit_peers(1, nf - 1, take_go)

    visit_peers(1, nf, lambda j: wait_into(at_in.at[j], at_recv.at[j]))

    part = width // CHUNKS
    core_rows, y_rows, x_rows = rows // 2, rows // 4, rows // 8
    core_base = pl.multiple_of(core * core_rows, core_rows)
    core_other = pl.multiple_of((1 - core) * core_rows, core_rows)
    y_base = pl.multiple_of(half * y_rows, y_rows)
    y_other = pl.multiple_of((1 - half) * y_rows, y_rows)
    x_base = pl.multiple_of(s * x_rows, x_rows)
    x_other = pl.multiple_of((1 - s) * x_rows, x_rows)

    def reduce_copy(stage, c):
        src, dst, device = (
            (core_out, core_in, sibling),
            (y_out, y_in, across),
            (x_out, x_in, partner),
        )[stage]
        return remote(src.at[c], dst.at[c], rs_send.at[stage, c], rs_recv.at[stage, c], device)

    def gather_copy(stage, c):
        base, count, device = (
            (core_base, core_rows, sibling),
            (core_base + y_base, y_rows, across),
            (core_base + y_base + x_base, x_rows, partner),
        )[stage]
        block = final.at[c, pl.ds(pl.multiple_of(base, count), count)]
        return remote(block, block, ag_send.at[stage, c], ag_recv.at[stage, c], device)

    for c in range(CHUNKS):
        acc[c] = dot_tn(
            at_in[...].reshape(nf * tokens, rows),
            cot[:, :, c * part : (c + 1) * part].reshape(nf * tokens, part),
        )
        core_out[c] = acc[c, pl.ds(core_other, core_rows)].astype(BF16)
        reduce_copy(0, c).start()

    def reduce_core(c):
        reduce_copy(0, c).wait_recv()
        acc[c, pl.ds(core_base, core_rows)] += core_in[c].astype(F32)
        y_out[c] = acc[c, pl.ds(core_base + y_other, y_rows)].astype(BF16)
        reduce_copy(1, c).start()

    def reduce_y(c):
        reduce_copy(1, c).wait_recv()
        acc[c, pl.ds(core_base + y_base, y_rows)] += y_in[c].astype(F32)
        x_out[c] = acc[c, pl.ds(core_base + y_base + x_other, x_rows)].astype(BF16)
        reduce_copy(2, c).start()

    def reduce_x(c):
        reduce_copy(2, c).wait_recv()
        mine = pl.ds(core_base + y_base + x_base, x_rows)
        final[c, mine] = (acc[c, mine] + x_in[c].astype(F32)).astype(BF16)
        gather_copy(2, c).start()

    def gather_x(c):
        gather_copy(2, c).wait()
        gather_copy(1, c).start()

    def gather_y(c):
        gather_copy(1, c).wait()
        gather_copy(0, c).start()

    def gather_core(c):
        gather_copy(0, c).wait()
        wg_ref[:, c * part : (c + 1) * part] = final[c]

    for c in range(CHUNKS):
        reduce_core(c)

    visit_peers(nf - 1, nf, take_go)

    for stage in (reduce_y, reduce_x, gather_x, gather_y):
        for c in range(CHUNKS):
            stage(c)

    def finish(g):
        cols = pl.ds(pl.multiple_of(g * rows, rows), rows)
        for which, out in ((0, kg_ref), (1, vg_ref)):
            kv_copy(which, g).wait()
            out[:, cols] = (kv_own[which, g] + kv_in[which, g].astype(F32)).astype(BF16)

    finish(f)
    visit_peers(1, nf, finish)

    for c in range(CHUNKS):
        gather_core(c)
        for stage in range(3):
            reduce_copy(stage, c).wait_send()

    def drain(j):
        go_copy(j, j).wait_send()
        at_copy(j, j).wait_send()

        @pl.when((j < f) & (f + 1 < nf))
        def _():
            cot_up(j).wait_send()

        @pl.when((j > f) & (f > 0))
        def _():
            cot_down(j).wait_send()

    visit_peers(1, nf, drain)

    @pl.when(f + 1 < nf)
    def _():
        cot_up(f).wait_send()

    @pl.when(f > 0)
    def _():
        cot_down(f).wait_send()


def fused_body(nf, queries, key_rows, value_rows, cotangent, out_weight):
    samples = lax.axis_size("dp") * nf
    tokens, heads_width = queries.shape[1:]
    rows, width = out_weight.shape
    part = width // CHUNKS
    vmem = pl.BlockSpec(memory_space=pltpu.VMEM)
    dma = pltpu.SemaphoreType.DMA
    outs = pl.pallas_call(
        functools.partial(fused_kernel, nf),
        out_shape=(
            jax.ShapeDtypeStruct((tokens, heads_width), BF16),
            jax.ShapeDtypeStruct((tokens, heads_width), BF16),
            jax.ShapeDtypeStruct((tokens, heads_width), BF16),
            jax.ShapeDtypeStruct((rows, width), BF16),
        ),
        in_specs=[vmem] * 5,
        out_specs=[vmem] * 4,
        scratch_shapes=[
            pltpu.VMEM((nf, tokens, width), BF16),
            pltpu.VMEM((2, tokens, heads_width), BF16),
            pltpu.VMEM((2, tokens, heads_width), BF16),
            pltpu.VMEM((nf, tokens, rows), BF16),
            pltpu.VMEM((nf, tokens, rows), BF16),
            pltpu.VMEM((nf, tokens, rows), BF16),
            pltpu.VMEM((nf, tokens, rows), BF16),
            pltpu.VMEM((heads_width // DH, tokens, 2 * tokens), F32),
            pltpu.VMEM((2, nf, tokens, rows), BF16),
            pltpu.VMEM((2, nf, tokens, rows), BF16),
            pltpu.VMEM((2, nf, tokens, rows), F32),
            pltpu.VMEM((CHUNKS, rows, part), F32),
            pltpu.VMEM((CHUNKS, rows // 2, part), BF16),
            pltpu.VMEM((CHUNKS, rows // 2, part), BF16),
            pltpu.VMEM((CHUNKS, rows // 4, part), BF16),
            pltpu.VMEM((CHUNKS, rows // 4, part), BF16),
            pltpu.VMEM((CHUNKS, rows // 8, part), BF16),
            pltpu.VMEM((CHUNKS, rows // 8, part), BF16),
            pltpu.VMEM((CHUNKS, rows, part), BF16),
            dma((2, nf)),
            dma((nf,)),
            dma((2,)),
            dma((2,)),
            dma((nf,)),
            dma((nf,)),
            dma((nf,)),
            dma((nf,)),
            dma((2, nf)),
            dma((2, nf)),
            dma((3, CHUNKS)),
            dma((3, CHUNKS)),
            dma((3, CHUNKS)),
            dma((3, CHUNKS)),
        ],
        compiler_params=pltpu.CompilerParams(
            collective_id=0, has_side_effects=True, vmem_limit_bytes=48 * 1024 * 1024
        ),
    )(queries[0], key_rows[0], value_rows[0], cotangent[0], out_weight)
    return (outs[0][None], outs[1][None], outs[2][None], outs[3].astype(F32) / samples)


def pick_body(mesh):
    if mesh.shape["seq"] == 2 and mesh.shape["dp"] == 4:
        return functools.partial(fused_body, mesh.shape["fsdp"])
    return body


def solution(mesh):
    return jax.shard_map(
        pick_body(mesh),
        mesh=mesh,
        in_specs=(
            P(("dp", "fsdp"), "seq", None),
            P(("dp", "fsdp"), "seq", None),
            P(("dp", "fsdp"), "seq", None),
            P(("dp", "fsdp"), "seq", None),
            P("fsdp", None),
        ),
        out_specs=(
            P(("dp", "fsdp"), "seq", None),
            P(("dp", "fsdp"), "seq", None),
            P(("dp", "fsdp"), "seq", None),
            P("fsdp", None),
        ),
        check_vma=False,
    )
```

```python
import functools

import jax
import jax.numpy as jnp
from jax import lax
from jax.experimental import pallas as pl
from jax.experimental.pallas import tpu as pltpu
from jax.sharding import PartitionSpec as P

DH = 128
CHUNKS = 4
X_FIRST = (3,)
STORES = 8
F32 = jnp.float32
BF16 = jnp.bfloat16


def head_backward(query_head, key_head, value_head, grad_head, block_rows):
    length = key_head.shape[0]
    score_scale = DH ** (-0.5)
    blocks = length // block_rows

    def visit(carry, block):
        key_acc, value_acc = carry
        begin = block * block_rows
        query_block = lax.dynamic_slice_in_dim(query_head, begin, block_rows, 0)
        grad_block = lax.dynamic_slice_in_dim(grad_head, begin, block_rows, 0)
        scores = (
            jnp.einsum("qd,kd->qk", query_block, key_head, preferred_element_type=jnp.float32)
            * score_scale
        )
        highest = jnp.max(scores, axis=1, keepdims=True)
        expanded = jnp.exp(scores - highest)
        weights = expanded / jnp.sum(expanded, axis=1, keepdims=True)
        weights_half = weights.astype(jnp.bfloat16)
        attended = jnp.einsum(
            "qk,kd->qd", weights_half, value_head, preferred_element_type=jnp.float32
        ).astype(jnp.bfloat16)
        grad_weights = jnp.einsum(
            "qd,kd->qk", grad_block, value_head, preferred_element_type=jnp.float32
        )
        row_delta = jnp.sum(weights * grad_weights, axis=1, keepdims=True)
        grad_scores = (weights * (grad_weights - row_delta)).astype(jnp.bfloat16)
        query_grad = (
            jnp.einsum("qk,kd->qd", grad_scores, key_head, preferred_element_type=jnp.float32)
            * score_scale
        ).astype(jnp.bfloat16)
        key_acc = key_acc + jnp.einsum(
            "qk,qd->kd", grad_scores, query_block, preferred_element_type=jnp.float32
        )
        value_acc = value_acc + jnp.einsum(
            "qk,qd->kd", weights_half, grad_block, preferred_element_type=jnp.float32
        )
        return ((key_acc, value_acc), (attended, query_grad))

    empty = jnp.zeros(key_head.shape, jnp.float32)
    finals, stacked = lax.scan(visit, (empty, empty), jnp.arange(blocks))
    attended = stacked[0].reshape(length, DH)
    query_grad = stacked[1].reshape(length, DH)
    key_grad = (finals[0] * score_scale).astype(jnp.bfloat16)
    value_grad = finals[1].astype(jnp.bfloat16)
    return (attended, query_grad, key_grad, value_grad)


def attend_heads(query_heads, key_heads, value_heads, grad_heads):
    length = query_heads.shape[1]
    per_device = query_heads.shape[2] // DH
    block_rows = min(512, length)
    gathered = [[], [], [], []]
    for head_index in range(per_device):
        lower = head_index * DH
        upper = lower + DH
        results = head_backward(
            query_heads[0, :, lower:upper],
            key_heads[0, :, lower:upper],
            value_heads[0, :, lower:upper],
            grad_heads[0, :, lower:upper],
            block_rows,
        )
        for position, result in enumerate(results):
            gathered[position].append(result)
    return tuple((jnp.concatenate(group, axis=1)[None] for group in gathered))


def body(queries, key_rows, value_rows, cotangent, out_weight):
    samples = lax.axis_size("dp") * lax.axis_size("fsdp")
    grad_out = jnp.einsum(
        "btd,rd->btr",
        cotangent,
        lax.all_gather(out_weight, "fsdp", axis=0, tiled=True),
        preferred_element_type=jnp.float32,
    ).astype(jnp.bfloat16)
    query_heads, key_heads, value_heads, grad_heads = (
        lax.all_to_all(queries, "seq", split_axis=2, concat_axis=1, tiled=True),
        lax.all_to_all(key_rows, "seq", split_axis=2, concat_axis=1, tiled=True),
        lax.all_to_all(value_rows, "seq", split_axis=2, concat_axis=1, tiled=True),
        lax.all_to_all(grad_out, "seq", split_axis=2, concat_axis=1, tiled=True),
    )
    head_results = attend_heads(query_heads, key_heads, value_heads, grad_heads)
    attended, query_grad, key_grad, value_grad = (
        lax.all_to_all(head_results[0], "seq", split_axis=1, concat_axis=2, tiled=True),
        lax.all_to_all(head_results[1], "seq", split_axis=1, concat_axis=2, tiled=True),
        lax.all_to_all(head_results[2], "seq", split_axis=1, concat_axis=2, tiled=True),
        lax.all_to_all(head_results[3], "seq", split_axis=1, concat_axis=2, tiled=True),
    )
    shares = lax.psum_scatter(
        jnp.einsum("btr,btd->rd", attended, cotangent, preferred_element_type=jnp.float32),
        ("fsdp", "seq"),
        scatter_dimension=0,
        tiled=True,
    )
    shares = lax.psum(shares.astype(jnp.bfloat16), "dp").astype(jnp.float32)
    total = lax.all_gather(shares.astype(jnp.bfloat16), "seq", axis=0, tiled=True).astype(
        shares.dtype
    )
    return (query_grad, key_grad, value_grad, total / samples)


def dot_nn(a, b):
    return lax.dot_general(a, b, (((1,), (0,)), ((), ())), preferred_element_type=F32)


def dot_nt(a, b):
    return lax.dot_general(a, b, (((1,), (1,)), ((), ())), preferred_element_type=F32)


def dot_tn(a, b):
    return lax.dot_general(a, b, (((0,), (0,)), ((), ())), preferred_element_type=F32)


def fused_kernel(
    nf,
    q_hbm,
    k_hbm,
    v_hbm,
    c_hbm,
    w_hbm,
    qg_hbm,
    kg_hbm,
    vg_hbm,
    wg_hbm,
    cot,
    keys,
    vals,
    go_out,
    go_in,
    at_out,
    at_in,
    probs,
    kv_out,
    kv_in,
    kv_own,
    acc,
    core_out,
    core_in,
    y_out,
    y_in,
    x_out,
    x_in,
    final,
    q_ref,
    w_ref,
    qg_ref,
    kg_ref,
    vg_ref,
    load_sem,
    store_sem,
    wide_sem,
    cot_send,
    cot_recv,
    pair_send,
    pair_recv,
    go_send,
    go_recv,
    at_send,
    at_recv,
    kv_send,
    kv_recv,
    rs_send,
    rs_recv,
    ag_send,
    ag_recv,
):
    tokens, width = c_hbm.shape
    rows = w_ref.shape[0]
    group_heads = rows // DH
    scale = DH ** (-0.5)
    dp = lax.axis_index("dp")
    f = lax.axis_index("fsdp")
    s = lax.axis_index("seq")
    core = dp % 2
    half = dp // 2
    sibling = {"dp": half * 2 + (1 - core)}
    across = {"dp": (1 - half) * 2 + core}
    partner = {"seq": 1 - s}

    def remote(src, dst, send, recv, device):
        return pltpu.make_async_remote_copy(
            src_ref=src,
            dst_ref=dst,
            send_sem=send,
            recv_sem=recv,
            device_id=device,
            device_id_type=pl.DeviceIdType.MESH,
        )

    loads = [
        pltpu.make_async_copy(src, dst, load_sem.at[i])
        for i, (src, dst) in enumerate(
            (
                (c_hbm, cot.at[f]),
                (w_hbm, w_ref),
                (k_hbm, keys.at[0]),
                (v_hbm, vals.at[0]),
                (q_hbm, q_ref),
            )
        )
    ]
    for load in loads:
        load.start()

    barrier = pltpu.get_barrier_semaphore()
    for device in (sibling, across, partner):
        pl.semaphore_signal(
            barrier, inc=1, device_id=device, device_id_type=pl.DeviceIdType.MESH
        )
    for step in range(1, nf):
        pl.semaphore_signal(
            barrier,
            inc=1,
            device_id={"fsdp": (f + step) % nf},
            device_id_type=pl.DeviceIdType.MESH,
        )
    pl.semaphore_wait(barrier, 3 + nf - 1)

    def cot_up(j):
        return remote(cot.at[j], cot.at[j], cot_send.at[0, j], cot_recv.at[j], {"fsdp": f + 1})

    def cot_down(j):
        return remote(cot.at[j], cot.at[j], cot_send.at[1, j], cot_recv.at[j], {"fsdp": f - 1})

    def go_copy(j, peer):
        return remote(go_out.at[j], go_in.at[f], go_send.at[j], go_recv.at[f], {"fsdp": peer})

    def at_copy(j, peer):
        return remote(at_out.at[j], at_in.at[f], at_send.at[j], at_recv.at[f], {"fsdp": peer})

    def kv_copy(which, g):
        return remote(
            kv_out.at[which, g],
            kv_in.at[which, g],
            kv_send.at[which, g],
            kv_recv.at[which, g],
            partner,
        )

    def wait_into(ref, sem):
        pltpu.make_async_copy(ref, ref, sem).wait()

    own_up = remote(c_hbm, cot.at[f], cot_send.at[0, f], cot_recv.at[f], {"fsdp": f + 1})
    own_down = remote(c_hbm, cot.at[f], cot_send.at[1, f], cot_recv.at[f], {"fsdp": f - 1})

    @pl.when(f + 1 < nf)
    def _():
        own_up.start()

    @pl.when(f > 0)
    def _():
        own_down.start()

    def pair_copy(which, i):
        g = (f + 1 + i) % nf
        cols = pl.ds(pl.multiple_of(g * rows, rows), rows)
        src, dst = ((k_hbm, keys), (v_hbm, vals))[which]
        return remote(
            src.at[:, cols],
            dst.at[1, :, cols],
            pair_send.at[which, i],
            pair_recv.at[which, i],
            partner,
        )

    for i in range(nf):
        pair_copy(0, i).start()
        pair_copy(1, i).start()

    def project(j):
        return dot_nt(cot[j], w_ref[...]).astype(BF16)

    loads[0].wait()
    loads[1].wait()
    go_in[f] = project(f)

    def visit_peers(first, last, action):
        def step(i, carry):
            d = i // 2
            j = f + d * (1 - 2 * (i % 2))

            @pl.when((j >= 0) & (j < nf))
            def _():
                action(j)

            return carry

        lax.fori_loop(2 * first, 2 * last, step, 0)

    def take_cot(j):
        wait_into(cot.at[j], cot_recv.at[j])

        @pl.when((j < f) & (f + 1 < nf))
        def _():
            cot_up(j).start()

        @pl.when((j > f) & (f > 0))
        def _():
            cot_down(j).start()

        go_out[j] = project(j)
        go_copy(j, j).start()

    def soften(i):
        g = (f + 1 + i) % nf
        base = g * rows
        pair_copy(0, i).wait()
        pair_copy(1, i).wait()
        for t in range(group_heads):
            cols = pl.ds(pl.multiple_of(base + t * DH, DH), DH)
            kh = keys[:, :, cols].reshape(2 * tokens, DH)
            vh = vals[:, :, cols].reshape(2 * tokens, DH)
            scores = dot_nt(q_ref[:, cols], kh) * scale
            highest = jnp.max(scores, axis=1, keepdims=True)
            expanded = jnp.exp(scores - highest)
            weights = expanded / jnp.sum(expanded, axis=1, keepdims=True)
            probs[g * group_heads + t] = weights
            at_out[g, :, t * DH : (t + 1) * DH] = dot_nn(weights.astype(BF16), vh).astype(BF16)

        if i == nf - 1:
            at_in[f] = at_out[f]
        else:
            at_copy(g, g).start()


    def differentiate(g):
        base = g * rows
        for t in range(group_heads):
            cols = pl.ds(pl.multiple_of(base + t * DH, DH), DH)
            inner = slice(t * DH, (t + 1) * DH)
            kh = keys[:, :, cols].reshape(2 * tokens, DH)
            vh = vals[:, :, cols].reshape(2 * tokens, DH)
            qh = q_ref[:, cols]
            gh = go_in[g, :, inner]
            weights = probs[g * group_heads + t]
            grad_weights = dot_nt(gh, vh)
            delta = jnp.sum(weights * grad_weights, axis=1, keepdims=True)
            grad_scores = (weights * (grad_weights - delta)).astype(BF16)
            qg_ref[:, cols] = (dot_nn(grad_scores, kh) * scale).astype(BF16)
            kg = dot_tn(grad_scores, qh) * scale
            vg = dot_tn(weights.astype(BF16), gh)
            kv_own[0, g, :, inner] = kg[:tokens]
            kv_own[1, g, :, inner] = vg[:tokens]
            kv_out[0, g, :, inner] = kg[tokens:].astype(BF16)
            kv_out[1, g, :, inner] = vg[tokens:].astype(BF16)
        kv_copy(0, g).start()
        kv_copy(1, g).start()

    def take_go(j):
        wait_into(go_in.at[j], go_recv.at[j])
        differentiate(j)

    for load in loads[2:]:
        load.wait()
    soften(0)
    for d in range(1, nf):
        visit_peers(d, d + 1, take_cot)
        soften(d)
    differentiate(f)
    visit_peers(1, nf - 1, take_go)

    visit_peers(1, nf, lambda j: wait_into(at_in.at[j], at_recv.at[j]))

    part = width // CHUNKS
    core_rows, mid_rows, low_rows = rows // 2, rows // 4, rows // 8

    def bases(c):
        first, second = (s, half) if c in X_FIRST else (half, s)
        mid = core * core_rows + first * mid_rows
        mid_other = core * core_rows + (1 - first) * mid_rows
        low = mid + second * low_rows
        low_other = mid + (1 - second) * low_rows
        return mid, mid_other, low, low_other

    def span(base, count):
        return pl.ds(pl.multiple_of(base, count), count)

    def device_of(stage, c):
        if stage == 0:
            return sibling
        return partner if (stage == 1) == (c in X_FIRST) else across

    def reduce_copy(stage, c):
        src, dst = ((core_out, core_in), (y_out, y_in), (x_out, x_in))[stage]
        device = device_of(stage, c)
        return remote(src.at[c], dst.at[c], rs_send.at[stage, c], rs_recv.at[stage, c], device)

    def gather_copy(stage, c):
        base, count = (
            (core * core_rows, core_rows),
            (bases(c)[0], mid_rows),
            (bases(c)[2], low_rows),
        )[stage]
        block = final.at[c, span(base, count)]
        device = device_of(stage, c)
        return remote(block, block, ag_send.at[stage, c], ag_recv.at[stage, c], device)

    at_all = at_in[...].reshape(nf * tokens, rows)

    for c in range(CHUNKS):
        acc[c] = dot_tn(at_all, cot[:, :, c * part : (c + 1) * part].reshape(nf * tokens, part))
        core_out[c] = acc[c, span((1 - core) * core_rows, core_rows)].astype(BF16)
        reduce_copy(0, c).start()

    def reduce_core(c):
        mid, mid_other, low, low_other = bases(c)
        reduce_copy(0, c).wait_recv()
        there = mid_other - core * core_rows
        y_out[c] = (
            acc[c, span(mid_other, mid_rows)] + core_in[c, span(there, mid_rows)].astype(F32)
        ).astype(BF16)
        reduce_copy(1, c).start()
        here = mid - core * core_rows
        acc[c, span(mid, mid_rows)] += core_in[c, span(here, mid_rows)].astype(F32)

    def reduce_y(c):
        mid, mid_other, low, low_other = bases(c)
        reduce_copy(1, c).wait_recv()
        acc[c, span(mid, mid_rows)] += y_in[c].astype(F32)
        x_out[c] = acc[c, span(low_other, low_rows)].astype(BF16)
        reduce_copy(2, c).start()

    def reduce_x(c):
        low = bases(c)[2]
        reduce_copy(2, c).wait_recv()
        mine = span(low, low_rows)
        final[c, mine] = (acc[c, mine] + x_in[c].astype(F32)).astype(BF16)
        gather_copy(2, c).start()

    def gather_x(c):
        gather_copy(2, c).wait()
        gather_copy(1, c).start()

    def gather_y(c):
        gather_copy(1, c).wait()
        gather_copy(0, c).start()

    def wide_copy(c):
        cols = slice(c * part, (c + 1) * part)
        return pltpu.make_async_copy(final.at[c], wg_hbm.at[:, cols], wide_sem.at[c])

    def gather_core(c):
        gather_copy(0, c).wait()
        wide_copy(c).start()

    def finish(g):
        cols = pl.ds(pl.multiple_of(g * rows, rows), rows)
        for which, out in ((0, kg_ref), (1, vg_ref)):
            kv_copy(which, g).wait()
            out[:, cols] = (kv_own[which, g] + kv_in[which, g].astype(F32)).astype(BF16)

    stores = [
        pltpu.make_async_copy(src, dst, store_sem.at[i])
        for i, (src, dst) in enumerate(((qg_ref, qg_hbm), (kg_ref, kg_hbm), (vg_ref, vg_hbm)))
    ]

    def finish_all():
        finish(f)
        visit_peers(1, nf, finish)
        for store in stores:
            store.start()

    visit_peers(nf - 1, nf, take_go)

    stages = (reduce_core, reduce_y, reduce_x, gather_x, gather_y, gather_core)
    for t in range(CHUNKS + len(stages) - 1):
        for stage in reversed(range(len(stages))):
            if 0 <= t - stage < CHUNKS:
                stages[stage](t - stage)
        if t == CHUNKS:
            finish_all()

    for c in range(CHUNKS):
        wide_copy(c).wait()
        for stage in range(3):
            reduce_copy(stage, c).wait_send()

    for store in stores:
        store.wait()

    def drain(j):
        go_copy(j, j).wait_send()
        at_copy(j, j).wait_send()

        @pl.when((j < f) & (f + 1 < nf))
        def _():
            cot_up(j).wait_send()

        @pl.when((j > f) & (f > 0))
        def _():
            cot_down(j).wait_send()

    visit_peers(1, nf, drain)

    @pl.when(f + 1 < nf)
    def _():
        own_up.wait_send()

    @pl.when(f > 0)
    def _():
        own_down.wait_send()


def store_kernel(
    factor, qg, kg, vg, wg, qg_out, kg_out, vg_out, wg_out, narrow, wide, sems, in_sems, out_sems
):
    count = wg.shape[0] // STORES
    blocks = [slice(i * count, (i + 1) * count) for i in range(STORES)]
    loads = [
        pltpu.make_async_copy(wg.at[block], narrow.at[block], in_sems.at[i])
        for i, block in enumerate(blocks)
    ]
    copies = [
        pltpu.make_async_copy(src, dst, sems.at[i])
        for i, (src, dst) in enumerate(((qg, qg_out), (kg, kg_out), (vg, vg_out)))
    ]
    for copy in loads + copies:
        copy.start()
    for i, block in enumerate(blocks):
        loads[i].wait()
        wide[block, :] = narrow[block, :].astype(F32) * factor
        copy = pltpu.make_async_copy(wide.at[block], wg_out.at[block], out_sems.at[i])
        copy.start()
        copies.append(copy)
    for copy in copies:
        copy.wait()


def fused_body(nf, queries, key_rows, value_rows, cotangent, out_weight):
    samples = lax.axis_size("dp") * nf
    tokens, heads_width = queries.shape[1:]
    rows, width = out_weight.shape
    part = width // CHUNKS
    dma = pltpu.SemaphoreType.DMA
    outs = pl.pallas_call(
        functools.partial(fused_kernel, nf),
        out_shape=(
            jax.ShapeDtypeStruct((tokens, heads_width), BF16),
            jax.ShapeDtypeStruct((tokens, heads_width), BF16),
            jax.ShapeDtypeStruct((tokens, heads_width), BF16),
            jax.ShapeDtypeStruct((rows, width), BF16),
        ),
        in_specs=[pl.BlockSpec(memory_space=pltpu.HBM)] * 5,
        out_specs=[pl.BlockSpec(memory_space=pltpu.HBM)] * 4,
        scratch_shapes=[
            pltpu.VMEM((nf, tokens, width), BF16),
            pltpu.VMEM((2, tokens, heads_width), BF16),
            pltpu.VMEM((2, tokens, heads_width), BF16),
            pltpu.VMEM((nf, tokens, rows), BF16),
            pltpu.VMEM((nf, tokens, rows), BF16),
            pltpu.VMEM((nf, tokens, rows), BF16),
            pltpu.VMEM((nf, tokens, rows), BF16),
            pltpu.VMEM((heads_width // DH, tokens, 2 * tokens), F32),
            pltpu.VMEM((2, nf, tokens, rows), BF16),
            pltpu.VMEM((2, nf, tokens, rows), BF16),
            pltpu.VMEM((2, nf, tokens, rows), F32),
            pltpu.VMEM((CHUNKS, rows, part), F32),
            pltpu.VMEM((CHUNKS, rows // 2, part), BF16),
            pltpu.VMEM((CHUNKS, rows // 2, part), BF16),
            pltpu.VMEM((CHUNKS, rows // 4, part), BF16),
            pltpu.VMEM((CHUNKS, rows // 4, part), BF16),
            pltpu.VMEM((CHUNKS, rows // 8, part), BF16),
            pltpu.VMEM((CHUNKS, rows // 8, part), BF16),
            pltpu.VMEM((CHUNKS, rows, part), BF16),
            pltpu.VMEM((tokens, heads_width), BF16),
            pltpu.VMEM((rows, width), BF16),
            pltpu.VMEM((tokens, heads_width), BF16),
            pltpu.VMEM((tokens, heads_width), BF16),
            pltpu.VMEM((tokens, heads_width), BF16),
            dma((5,)),
            dma((3,)),
            dma((CHUNKS,)),
            dma((2, nf)),
            dma((nf,)),
            dma((2, nf)),
            dma((2, nf)),
            dma((nf,)),
            dma((nf,)),
            dma((nf,)),
            dma((nf,)),
            dma((2, nf)),
            dma((2, nf)),
            dma((3, CHUNKS)),
            dma((3, CHUNKS)),
            dma((3, CHUNKS)),
            dma((3, CHUNKS)),
        ],
        compiler_params=pltpu.CompilerParams(
            collective_id=0, has_side_effects=True, vmem_limit_bytes=58 * 1024 * 1024
        ),
    )(queries[0], key_rows[0], value_rows[0], cotangent[0], out_weight)
    stored = pl.pallas_call(
        functools.partial(store_kernel, 1.0 / samples),
        out_shape=tuple(jax.ShapeDtypeStruct(out.shape, out.dtype) for out in outs[:3])
        + (jax.ShapeDtypeStruct((rows, width), F32),),
        in_specs=[pl.BlockSpec(memory_space=pltpu.HBM)] * 4,
        out_specs=[pl.BlockSpec(memory_space=pltpu.HBM)] * 4,
        scratch_shapes=[
            pltpu.VMEM((rows, width), BF16),
            pltpu.VMEM((rows, width), F32),
            dma((3,)),
            dma((STORES,)),
            dma((STORES,)),
        ],
        compiler_params=pltpu.CompilerParams(vmem_limit_bytes=58 * 1024 * 1024),
    )(*outs)
    return tuple(out[None] for out in stored[:3]) + (stored[3],)


def pick_body(mesh):
    if mesh.shape["seq"] == 2 and mesh.shape["dp"] == 4:
        return functools.partial(fused_body, mesh.shape["fsdp"])
    return body


def solution(mesh):
    return jax.shard_map(
        pick_body(mesh),
        mesh=mesh,
        in_specs=(
            P(("dp", "fsdp"), "seq", None),
            P(("dp", "fsdp"), "seq", None),
            P(("dp", "fsdp"), "seq", None),
            P(("dp", "fsdp"), "seq", None),
            P("fsdp", None),
        ),
        out_specs=(
            P(("dp", "fsdp"), "seq", None),
            P(("dp", "fsdp"), "seq", None),
            P(("dp", "fsdp"), "seq", None),
            P("fsdp", None),
        ),
        check_vma=False,
    )
```

```python
import functools

import jax
import jax.numpy as jnp
from jax import lax
from jax.experimental import pallas as pl
from jax.experimental.pallas import tpu as pltpu
from jax.sharding import PartitionSpec as P

DH = 128
CHUNKS = 4
X_FIRST = (1, 3)
STORES = 8
F32 = jnp.float32
BF16 = jnp.bfloat16


def head_backward(query_head, key_head, value_head, grad_head, block_rows):
    length = key_head.shape[0]
    score_scale = DH ** (-0.5)
    blocks = length // block_rows

    def visit(carry, block):
        key_acc, value_acc = carry
        begin = block * block_rows
        query_block = lax.dynamic_slice_in_dim(query_head, begin, block_rows, 0)
        grad_block = lax.dynamic_slice_in_dim(grad_head, begin, block_rows, 0)
        scores = (
            jnp.einsum("qd,kd->qk", query_block, key_head, preferred_element_type=jnp.float32)
            * score_scale
        )
        highest = jnp.max(scores, axis=1, keepdims=True)
        expanded = jnp.exp(scores - highest)
        weights = expanded / jnp.sum(expanded, axis=1, keepdims=True)
        weights_half = weights.astype(jnp.bfloat16)
        attended = jnp.einsum(
            "qk,kd->qd", weights_half, value_head, preferred_element_type=jnp.float32
        ).astype(jnp.bfloat16)
        grad_weights = jnp.einsum(
            "qd,kd->qk", grad_block, value_head, preferred_element_type=jnp.float32
        )
        row_delta = jnp.sum(weights * grad_weights, axis=1, keepdims=True)
        grad_scores = (weights * (grad_weights - row_delta)).astype(jnp.bfloat16)
        query_grad = (
            jnp.einsum("qk,kd->qd", grad_scores, key_head, preferred_element_type=jnp.float32)
            * score_scale
        ).astype(jnp.bfloat16)
        key_acc = key_acc + jnp.einsum(
            "qk,qd->kd", grad_scores, query_block, preferred_element_type=jnp.float32
        )
        value_acc = value_acc + jnp.einsum(
            "qk,qd->kd", weights_half, grad_block, preferred_element_type=jnp.float32
        )
        return ((key_acc, value_acc), (attended, query_grad))

    empty = jnp.zeros(key_head.shape, jnp.float32)
    finals, stacked = lax.scan(visit, (empty, empty), jnp.arange(blocks))
    attended = stacked[0].reshape(length, DH)
    query_grad = stacked[1].reshape(length, DH)
    key_grad = (finals[0] * score_scale).astype(jnp.bfloat16)
    value_grad = finals[1].astype(jnp.bfloat16)
    return (attended, query_grad, key_grad, value_grad)


def attend_heads(query_heads, key_heads, value_heads, grad_heads):
    length = query_heads.shape[1]
    per_device = query_heads.shape[2] // DH
    block_rows = min(512, length)
    gathered = [[], [], [], []]
    for head_index in range(per_device):
        lower = head_index * DH
        upper = lower + DH
        results = head_backward(
            query_heads[0, :, lower:upper],
            key_heads[0, :, lower:upper],
            value_heads[0, :, lower:upper],
            grad_heads[0, :, lower:upper],
            block_rows,
        )
        for position, result in enumerate(results):
            gathered[position].append(result)
    return tuple((jnp.concatenate(group, axis=1)[None] for group in gathered))


def body(queries, key_rows, value_rows, cotangent, out_weight):
    samples = lax.axis_size("dp") * lax.axis_size("fsdp")
    grad_out = jnp.einsum(
        "btd,rd->btr",
        cotangent,
        lax.all_gather(out_weight, "fsdp", axis=0, tiled=True),
        preferred_element_type=jnp.float32,
    ).astype(jnp.bfloat16)
    query_heads, key_heads, value_heads, grad_heads = (
        lax.all_to_all(queries, "seq", split_axis=2, concat_axis=1, tiled=True),
        lax.all_to_all(key_rows, "seq", split_axis=2, concat_axis=1, tiled=True),
        lax.all_to_all(value_rows, "seq", split_axis=2, concat_axis=1, tiled=True),
        lax.all_to_all(grad_out, "seq", split_axis=2, concat_axis=1, tiled=True),
    )
    head_results = attend_heads(query_heads, key_heads, value_heads, grad_heads)
    attended, query_grad, key_grad, value_grad = (
        lax.all_to_all(head_results[0], "seq", split_axis=1, concat_axis=2, tiled=True),
        lax.all_to_all(head_results[1], "seq", split_axis=1, concat_axis=2, tiled=True),
        lax.all_to_all(head_results[2], "seq", split_axis=1, concat_axis=2, tiled=True),
        lax.all_to_all(head_results[3], "seq", split_axis=1, concat_axis=2, tiled=True),
    )
    shares = lax.psum_scatter(
        jnp.einsum("btr,btd->rd", attended, cotangent, preferred_element_type=jnp.float32),
        ("fsdp", "seq"),
        scatter_dimension=0,
        tiled=True,
    )
    shares = lax.psum(shares.astype(jnp.bfloat16), "dp").astype(jnp.float32)
    total = lax.all_gather(shares.astype(jnp.bfloat16), "seq", axis=0, tiled=True).astype(
        shares.dtype
    )
    return (query_grad, key_grad, value_grad, total / samples)


def dot_nn(a, b):
    return lax.dot_general(a, b, (((1,), (0,)), ((), ())), preferred_element_type=F32)


def dot_nt(a, b):
    return lax.dot_general(a, b, (((1,), (1,)), ((), ())), preferred_element_type=F32)


def dot_tn(a, b):
    return lax.dot_general(a, b, (((0,), (0,)), ((), ())), preferred_element_type=F32)


def fused_kernel(
    nf,
    q_hbm,
    k_hbm,
    v_hbm,
    c_hbm,
    w_hbm,
    qg_hbm,
    kg_hbm,
    vg_hbm,
    wg_hbm,
    cot,
    keys,
    vals,
    go_out,
    go_in,
    at_out,
    at_in,
    probs,
    kv_out,
    kv_in,
    kv_own,
    acc,
    core_out,
    core_in,
    y_out,
    y_in,
    x_out,
    x_in,
    final,
    q_ref,
    w_ref,
    qg_ref,
    kg_ref,
    vg_ref,
    load_sem,
    pair_sem,
    store_sem,
    wide_sem,
    cot_send,
    cot_recv,
    pair_send,
    pair_recv,
    go_send,
    go_recv,
    at_send,
    at_recv,
    kv_send,
    kv_recv,
    rs_send,
    rs_recv,
    ag_send,
    ag_recv,
):
    tokens, width = c_hbm.shape
    rows = w_ref.shape[0]
    group_heads = rows // DH
    scale = DH ** (-0.5)
    dp = lax.axis_index("dp")
    f = lax.axis_index("fsdp")
    s = lax.axis_index("seq")
    core = dp % 2
    half = dp // 2
    sibling = {"dp": half * 2 + (1 - core)}
    across = {"dp": (1 - half) * 2 + core}
    partner = {"seq": 1 - s}

    def remote(src, dst, send, recv, device):
        return pltpu.make_async_remote_copy(
            src_ref=src,
            dst_ref=dst,
            send_sem=send,
            recv_sem=recv,
            device_id=device,
            device_id_type=pl.DeviceIdType.MESH,
        )

    loads = [
        pltpu.make_async_copy(src, dst, load_sem.at[i])
        for i, (src, dst) in enumerate(
            (
                (c_hbm, cot.at[f]),
                (w_hbm, w_ref),
                (q_hbm, q_ref),
            )
        )
    ]

    def group_at(i):
        return (f + 1 + i) % nf

    def pair_load(which, i):
        g = group_at(i)
        cols = pl.ds(pl.multiple_of(g * rows, rows), rows)
        src, dst = ((k_hbm, keys), (v_hbm, vals))[which]
        return pltpu.make_async_copy(src.at[:, cols], dst.at[0, g], pair_sem.at[which, i])

    loads[0].start()
    for i in range(nf):
        pair_load(0, i).start()
        pair_load(1, i).start()
    loads[1].start()
    loads[2].start()

    barrier = pltpu.get_barrier_semaphore()
    for device in (sibling, across, partner):
        pl.semaphore_signal(
            barrier, inc=1, device_id=device, device_id_type=pl.DeviceIdType.MESH
        )
    for step in range(1, nf):
        pl.semaphore_signal(
            barrier,
            inc=1,
            device_id={"fsdp": (f + step) % nf},
            device_id_type=pl.DeviceIdType.MESH,
        )
    pl.semaphore_wait(barrier, 3 + nf - 1)

    def cot_up(j):
        return remote(cot.at[j], cot.at[j], cot_send.at[0, j], cot_recv.at[j], {"fsdp": f + 1})

    def cot_down(j):
        return remote(cot.at[j], cot.at[j], cot_send.at[1, j], cot_recv.at[j], {"fsdp": f - 1})

    def go_copy(j, peer):
        return remote(go_out.at[j], go_in.at[f], go_send.at[j], go_recv.at[f], {"fsdp": peer})

    def at_copy(j, peer):
        return remote(at_out.at[j], at_in.at[f], at_send.at[j], at_recv.at[f], {"fsdp": peer})

    def kv_copy(which, g):
        return remote(
            kv_out.at[which, g],
            kv_in.at[which, g],
            kv_send.at[which, g],
            kv_recv.at[which, g],
            partner,
        )

    def wait_into(ref, sem):
        pltpu.make_async_copy(ref, ref, sem).wait()

    loads[0].wait()

    @pl.when(f + 1 < nf)
    def _():
        cot_up(f).start()

    @pl.when(f > 0)
    def _():
        cot_down(f).start()

    def pair_copy(which, i):
        g = group_at(i)
        buffer = (keys, vals)[which]
        return remote(
            buffer.at[0, g],
            buffer.at[1, g],
            pair_send.at[which, i],
            pair_recv.at[which, i],
            partner,
        )

    for i in range(nf):
        for which in range(2):
            pair_load(which, i).wait()
            pair_copy(which, i).start()

    def project(j):
        return dot_nt(cot[j], w_ref[...]).astype(BF16)

    loads[1].wait()
    go_in[f] = project(f)

    def visit_peers(first, last, action):
        def step(i, carry):
            d = i // 2
            j = f + d * (1 - 2 * (i % 2))

            @pl.when((j >= 0) & (j < nf))
            def _():
                action(j)

            return carry

        lax.fori_loop(2 * first, 2 * last, step, 0)

    def take_cot(j):
        wait_into(cot.at[j], cot_recv.at[j])

        @pl.when((j < f) & (f + 1 < nf))
        def _():
            cot_up(j).start()

        @pl.when((j > f) & (f > 0))
        def _():
            cot_down(j).start()

        go_out[j] = project(j)
        go_copy(j, j).start()

    def soften(i):
        g = group_at(i)
        base = g * rows
        pair_copy(0, i).wait()
        pair_copy(1, i).wait()
        for t in range(group_heads):
            cols = pl.ds(pl.multiple_of(base + t * DH, DH), DH)
            inner = slice(t * DH, (t + 1) * DH)
            kh = keys[:, g, :, inner].reshape(2 * tokens, DH)
            vh = vals[:, g, :, inner].reshape(2 * tokens, DH)
            scores = dot_nt(q_ref[:, cols], kh) * scale
            highest = jnp.max(scores, axis=1, keepdims=True)
            expanded = jnp.exp(scores - highest)
            weights = expanded / jnp.sum(expanded, axis=1, keepdims=True)
            probs[g * group_heads + t] = weights
            at_out[g, :, t * DH : (t + 1) * DH] = dot_nn(weights.astype(BF16), vh).astype(BF16)

        if i == nf - 1:
            at_in[f] = at_out[f]
        else:
            at_copy(g, g).start()


    def differentiate(g):
        base = g * rows
        for t in range(group_heads):
            cols = pl.ds(pl.multiple_of(base + t * DH, DH), DH)
            inner = slice(t * DH, (t + 1) * DH)
            kh = keys[:, g, :, inner].reshape(2 * tokens, DH)
            vh = vals[:, g, :, inner].reshape(2 * tokens, DH)
            qh = q_ref[:, cols]
            gh = go_in[g, :, inner]
            weights = probs[g * group_heads + t]
            grad_weights = dot_nt(gh, vh)
            delta = jnp.sum(weights * grad_weights, axis=1, keepdims=True)
            grad_scores = (weights * (grad_weights - delta)).astype(BF16)
            qg_ref[:, cols] = (dot_nn(grad_scores, kh) * scale).astype(BF16)
            kg = dot_tn(grad_scores, qh) * scale
            vg = dot_tn(weights.astype(BF16), gh)
            kv_own[0, g, :, inner] = kg[:tokens]
            kv_own[1, g, :, inner] = vg[:tokens]
            kv_out[0, g, :, inner] = kg[tokens:].astype(BF16)
            kv_out[1, g, :, inner] = vg[tokens:].astype(BF16)
        kv_copy(0, g).start()
        kv_copy(1, g).start()

    def take_go(j):
        wait_into(go_in.at[j], go_recv.at[j])
        differentiate(j)

    loads[2].wait()
    visit_peers(1, nf - 1, take_cot)
    for d in range(nf):
        soften(d)
    differentiate(f)
    visit_peers(nf - 1, nf, take_cot)
    visit_peers(1, nf - 1, take_go)

    visit_peers(1, nf, lambda j: wait_into(at_in.at[j], at_recv.at[j]))

    part = width // CHUNKS
    core_rows, mid_rows, low_rows = rows // 2, rows // 4, rows // 8

    def bases(c):
        first, second = (s, half) if c in X_FIRST else (half, s)
        mid = core * core_rows + first * mid_rows
        mid_other = core * core_rows + (1 - first) * mid_rows
        low = mid + second * low_rows
        low_other = mid + (1 - second) * low_rows
        return mid, mid_other, low, low_other

    def span(base, count):
        return pl.ds(pl.multiple_of(base, count), count)

    def device_of(stage, c):
        if stage == 0:
            return sibling
        return partner if (stage == 1) == (c in X_FIRST) else across

    def reduce_copy(stage, c):
        src, dst = ((core_out, core_in), (y_out, y_in), (x_out, x_in))[stage]
        device = device_of(stage, c)
        return remote(src.at[c], dst.at[c], rs_send.at[stage, c], rs_recv.at[stage, c], device)

    def gather_copy(stage, c):
        base, count = (
            (core * core_rows, core_rows),
            (bases(c)[0], mid_rows),
            (bases(c)[2], low_rows),
        )[stage]
        block = final.at[c, span(base, count)]
        device = device_of(stage, c)
        return remote(block, block, ag_send.at[stage, c], ag_recv.at[stage, c], device)

    at_all = at_in[...].reshape(nf * tokens, rows)

    for c in range(CHUNKS):
        acc[c] = dot_tn(at_all, cot[:, :, c * part : (c + 1) * part].reshape(nf * tokens, part))
        core_out[c] = acc[c, span((1 - core) * core_rows, core_rows)].astype(BF16)
        reduce_copy(0, c).start()

    def reduce_core(c):
        mid, mid_other, low, low_other = bases(c)
        reduce_copy(0, c).wait_recv()
        there = mid_other - core * core_rows
        y_out[c] = (
            acc[c, span(mid_other, mid_rows)] + core_in[c, span(there, mid_rows)].astype(F32)
        ).astype(BF16)
        reduce_copy(1, c).start()
        here = mid - core * core_rows
        acc[c, span(mid, mid_rows)] += core_in[c, span(here, mid_rows)].astype(F32)

    def reduce_y(c):
        mid, mid_other, low, low_other = bases(c)
        reduce_copy(1, c).wait_recv()
        acc[c, span(mid, mid_rows)] += y_in[c].astype(F32)
        x_out[c] = acc[c, span(low_other, low_rows)].astype(BF16)
        reduce_copy(2, c).start()

    def reduce_x(c):
        low = bases(c)[2]
        reduce_copy(2, c).wait_recv()
        mine = span(low, low_rows)
        final[c, mine] = (acc[c, mine] + x_in[c].astype(F32)).astype(BF16)
        gather_copy(2, c).start()

    def gather_x(c):
        gather_copy(2, c).wait()
        gather_copy(1, c).start()

    def gather_y(c):
        gather_copy(1, c).wait()
        gather_copy(0, c).start()

    def wide_copy(c):
        cols = slice(c * part, (c + 1) * part)
        return pltpu.make_async_copy(final.at[c], wg_hbm.at[:, cols], wide_sem.at[c])

    def gather_core(c):
        gather_copy(0, c).wait()
        wide_copy(c).start()

    def finish(g):
        cols = pl.ds(pl.multiple_of(g * rows, rows), rows)
        for which, out in ((0, kg_ref), (1, vg_ref)):
            kv_copy(which, g).wait()
            out[:, cols] = (kv_own[which, g] + kv_in[which, g].astype(F32)).astype(BF16)

    stores = [
        pltpu.make_async_copy(src, dst, store_sem.at[i])
        for i, (src, dst) in enumerate(((qg_ref, qg_hbm), (kg_ref, kg_hbm), (vg_ref, vg_hbm)))
    ]

    def finish_all():
        finish(f)
        visit_peers(1, nf, finish)
        for store in stores:
            store.start()

    for c in range(CHUNKS):
        reduce_core(c)

    visit_peers(nf - 1, nf, take_go)

    for stage in (reduce_y, reduce_x, gather_x, gather_y):
        for c in range(CHUNKS):
            stage(c)

    finish_all()

    for c in range(CHUNKS):
        gather_core(c)

    for c in range(CHUNKS):
        wide_copy(c).wait()
        for stage in range(3):
            reduce_copy(stage, c).wait_send()

    for store in stores:
        store.wait()

    def drain(j):
        go_copy(j, j).wait_send()
        at_copy(j, j).wait_send()

        @pl.when((j < f) & (f + 1 < nf))
        def _():
            cot_up(j).wait_send()

        @pl.when((j > f) & (f > 0))
        def _():
            cot_down(j).wait_send()

    visit_peers(1, nf, drain)

    @pl.when(f + 1 < nf)
    def _():
        cot_up(f).wait_send()

    @pl.when(f > 0)
    def _():
        cot_down(f).wait_send()


def store_kernel(
    factor,
    qg,
    kg,
    vg,
    wg,
    qg_out,
    kg_out,
    vg_out,
    wg_out,
    held,
    narrow,
    wide,
    sems,
    in_sems,
    out_sems,
):
    count = wg.shape[0] // STORES
    blocks = [slice(i * count, (i + 1) * count) for i in range(STORES)]
    loads = [
        pltpu.make_async_copy(wg.at[block], narrow.at[block], in_sems.at[i])
        for i, block in enumerate(blocks)
    ]
    fills = [
        pltpu.make_async_copy(src, held.at[i], sems.at[0, i]) for i, src in enumerate((qg, kg, vg))
    ]
    copies = [
        pltpu.make_async_copy(held.at[i], dst, sems.at[1, i])
        for i, dst in enumerate((qg_out, kg_out, vg_out))
    ]
    for copy in loads + fills:
        copy.start()
    for i, block in enumerate(blocks):
        loads[i].wait()
        wide[block, :] = narrow[block, :].astype(F32) * factor
        pltpu.make_async_copy(wide.at[block], wg_out.at[block], out_sems.at[i]).start()
    for fill, copy in zip(fills, copies):
        fill.wait()
        copy.start()
    for i, block in enumerate(blocks):
        pltpu.make_async_copy(wide.at[block], wg_out.at[block], out_sems.at[i]).wait()
    for copy in copies:
        copy.wait()


def fused_body(nf, queries, key_rows, value_rows, cotangent, out_weight):
    samples = lax.axis_size("dp") * nf
    tokens, heads_width = queries.shape[1:]
    rows, width = out_weight.shape
    part = width // CHUNKS
    dma = pltpu.SemaphoreType.DMA
    outs = pl.pallas_call(
        functools.partial(fused_kernel, nf),
        out_shape=(
            jax.ShapeDtypeStruct((tokens, heads_width), BF16),
            jax.ShapeDtypeStruct((tokens, heads_width), BF16),
            jax.ShapeDtypeStruct((tokens, heads_width), BF16),
            jax.ShapeDtypeStruct((rows, width), BF16),
        ),
        in_specs=[pl.BlockSpec(memory_space=pltpu.HBM)] * 5,
        out_specs=[pl.BlockSpec(memory_space=pltpu.HBM)] * 4,
        scratch_shapes=[
            pltpu.VMEM((nf, tokens, width), BF16),
            pltpu.VMEM((2, nf, tokens, rows), BF16),
            pltpu.VMEM((2, nf, tokens, rows), BF16),
            pltpu.VMEM((nf, tokens, rows), BF16),
            pltpu.VMEM((nf, tokens, rows), BF16),
            pltpu.VMEM((nf, tokens, rows), BF16),
            pltpu.VMEM((nf, tokens, rows), BF16),
            pltpu.VMEM((heads_width // DH, tokens, 2 * tokens), F32),
            pltpu.VMEM((2, nf, tokens, rows), BF16),
            pltpu.VMEM((2, nf, tokens, rows), BF16),
            pltpu.VMEM((2, nf, tokens, rows), F32),
            pltpu.VMEM((CHUNKS, rows, part), F32),
            pltpu.VMEM((CHUNKS, rows // 2, part), BF16),
            pltpu.VMEM((CHUNKS, rows // 2, part), BF16),
            pltpu.VMEM((CHUNKS, rows // 4, part), BF16),
            pltpu.VMEM((CHUNKS, rows // 4, part), BF16),
            pltpu.VMEM((CHUNKS, rows // 8, part), BF16),
            pltpu.VMEM((CHUNKS, rows // 8, part), BF16),
            pltpu.VMEM((CHUNKS, rows, part), BF16),
            pltpu.VMEM((tokens, heads_width), BF16),
            pltpu.VMEM((rows, width), BF16),
            pltpu.VMEM((tokens, heads_width), BF16),
            pltpu.VMEM((tokens, heads_width), BF16),
            pltpu.VMEM((tokens, heads_width), BF16),
            dma((3,)),
            dma((2, nf)),
            dma((3,)),
            dma((CHUNKS,)),
            dma((2, nf)),
            dma((nf,)),
            dma((2, nf)),
            dma((2, nf)),
            dma((nf,)),
            dma((nf,)),
            dma((nf,)),
            dma((nf,)),
            dma((2, nf)),
            dma((2, nf)),
            dma((3, CHUNKS)),
            dma((3, CHUNKS)),
            dma((3, CHUNKS)),
            dma((3, CHUNKS)),
        ],
        compiler_params=pltpu.CompilerParams(
            collective_id=0, has_side_effects=True, vmem_limit_bytes=58 * 1024 * 1024
        ),
    )(queries[0], key_rows[0], value_rows[0], cotangent[0], out_weight)
    stored = pl.pallas_call(
        functools.partial(store_kernel, 1.0 / samples),
        out_shape=tuple(jax.ShapeDtypeStruct(out.shape, out.dtype) for out in outs[:3])
        + (jax.ShapeDtypeStruct((rows, width), F32),),
        in_specs=[pl.BlockSpec(memory_space=pltpu.HBM)] * 4,
        out_specs=[pl.BlockSpec(memory_space=pltpu.HBM)] * 4,
        scratch_shapes=[
            pltpu.VMEM((3, tokens, heads_width), BF16),
            pltpu.VMEM((rows, width), BF16),
            pltpu.VMEM((rows, width), F32),
            dma((2, 3)),
            dma((STORES,)),
            dma((STORES,)),
        ],
        compiler_params=pltpu.CompilerParams(vmem_limit_bytes=58 * 1024 * 1024),
    )(*outs)
    return tuple(out[None] for out in stored[:3]) + (stored[3],)


def pick_body(mesh):
    if mesh.shape["seq"] == 2 and mesh.shape["dp"] == 4:
        return functools.partial(fused_body, mesh.shape["fsdp"])
    return body


def solution(mesh):
    return jax.shard_map(
        pick_body(mesh),
        mesh=mesh,
        in_specs=(
            P(("dp", "fsdp"), "seq", None),
            P(("dp", "fsdp"), "seq", None),
            P(("dp", "fsdp"), "seq", None),
            P(("dp", "fsdp"), "seq", None),
            P("fsdp", None),
        ),
        out_specs=(
            P(("dp", "fsdp"), "seq", None),
            P(("dp", "fsdp"), "seq", None),
            P(("dp", "fsdp"), "seq", None),
            P("fsdp", None),
        ),
        check_vma=False,
    )
```
